128 devices in a mesh: row: 8 (over y, core), col: 16 (over z, x).
Axes of the slice: x: 4, y: 4, z: 4, core: 2. Of those that a mesh axis runs over, the one named last changes fastest.
Arguments:
- amplitudes: bfloat16 [16384, 32768], P('col', 'row'), may hold values from -6 to 6
- amp_mask: int32 [128, 256], P('col', 'row'), may hold values from 0 to 1, as said below
- integrals: bfloat16 [2, 4096, 10240], P(None, 'col', 'row'), may hold values from -0.09375 to 0.09375
- int_mask: int32 [2, 32, 80], P(None, 'col', 'row'), may hold values 0 or 1
- steps: int32 [2], replicated, may hold values from 0 to 7, as said below
Outputs:
- ladder: float32 [16384, 10240], P('col', 'row')
The draws below stay inside these ranges and needn't reach their ends.
Inputs may be any that keep to these rules, and one draw needn't show every extreme that they name: `steps`: distinct grid rows. `amp_mask`: split the 32 cd tile columns of one row device's panel into 16 aligned groups of 2; for every column device's 8 pair tile rows, exactly 1 tile columns of every group hold a nonzero tile; on some column devices every pair tile row of those columns is nonzero.
All inputs are finite; a program needn't handle non-finite values. No bound on the sum of `int_mask` on one device may be relied on, other than what follows from the above.
Results may differ from the reference program's by a relative error of at most 0.0003.
Values may be sent and summed in bfloat16 or wider, within the bound.
No kernel may reach another device: no remote copies, remote signals or barrier semaphores. Data moves between devices by JAX's collectives and lax.ppermute only.
A program may use at most 192 MiB of HBM per device.

```python
import jax
import jax.numpy as jnp
from jax import lax

TW = 128
PTD = 2
CAP = 1
STEPS = 2
OPT = 8
PT = 32
KP = 4096
M = 16384
NB = 10240
N_ROW = 8
N_COL = 16


def draw_amp_mask(key, part):
    key = jax.random.fold_in(key, 11)
    keys = jax.random.split(key, 3)
    scores = jax.random.randint(keys[0], (N_ROW, N_COL, N_COL, PTD), 0, 1 << 20) * PTD + jnp.arange(PTD)
    order = jnp.argsort(scores, axis=-1)
    ranks = jnp.argsort(order, axis=-1)
    needed = (ranks < CAP).reshape(N_ROW, N_COL, PT)
    coins = jax.random.randint(keys[1], (N_ROW, N_COL, OPT, PT), 0, 8) < 7
    anchor = jax.random.randint(keys[2], (N_ROW, N_COL, 1, PT), 0, OPT)
    row_ids = jnp.arange(N_ROW)[:, None, None, None]
    col_ids = jnp.arange(N_COL)[None, :, None, None]
    full = col_ids == row_ids % N_COL
    present = coins | (jnp.arange(OPT)[None, None, :, None] == anchor) | full
    result = needed[:, :, None, :] & present
    return result.transpose(1, 2, 0, 3).reshape(N_COL * OPT, N_ROW * PT).astype(jnp.int32)


def draw_steps(key, part):
    key = jax.random.fold_in(key, 7)
    keys = jax.random.split(key, 2)
    others = jax.random.permutation(keys[0], N_ROW - 1)[:STEPS - 1].astype(jnp.int32)
    values = jnp.concatenate([others, jnp.full((1,), N_ROW - 1, jnp.int32)])
    places = jax.random.permutation(keys[1], STEPS)
    return values[places].astype(jnp.int32)


def set_ends(entries, own_key, low, top_value):
    shape = entries.shape
    spot = [jax.random.randint(jax.random.fold_in(own_key, axis), (), 0, shape[axis]) for axis in range(len(shape))]
    entries = entries.at[tuple(spot)].set(low)
    longest = shape.index(max(shape))
    spot[longest] = (spot[longest] + 1) % shape[longest]
    return entries.at[tuple(spot)].set(top_value)


def steps_of(own_key, extent, pieces, low, top_value):
    def one(axis_at, parts):
        heights = jax.random.uniform(jax.random.fold_in(jax.random.fold_in(own_key, 6), axis_at), (parts,), jnp.float32, low / len(pieces), top_value / len(pieces))
        return jnp.repeat(jnp.exp(heights), extent[axis_at] // parts).reshape((-1,) + (1,) * (len(extent) - axis_at - 1))

    factor_of = one(*pieces[0])
    for cut in pieces[1:]:
        factor_of = factor_of * one(*cut)
    return factor_of


def gaussian(rng, shape, width, most, shards=(), dtype=jnp.bfloat16):
    entries = jax.random.normal(rng, shape, jnp.float32) * width
    if len(shards) > 0:
        entries = steps_of(rng, shape, shards, -0.22, 0.18) * entries
    return jnp.clip(entries, min=-most, max=most).astype(dtype)


def setup_inputs(seed: int = 0) -> dict:
    arg_keys = jax.random.split(jax.random.key(seed), 6)
    amplitudes = gaussian(arg_keys[0], (M, KP * N_ROW), 1.0, 6.0, ((0, 16), (1, 8)))
    amp_mask = draw_amp_mask(jax.random.fold_in(arg_keys[5], 71), 0)
    integrals = gaussian(arg_keys[2], (STEPS, KP, NB), KP ** -0.5, 0.09375, ((1, 16), (2, 8)))
    int_mask = set_ends((jax.random.randint(arg_keys[3], (STEPS, PT, NB // TW), 0, 4) < 3).astype(jnp.int32), jax.random.fold_in(arg_keys[3], 1), 0, 1)
    steps = draw_steps(jax.random.fold_in(arg_keys[5], 71), 0)
    return dict(amplitudes=amplitudes, amp_mask=amp_mask, integrals=integrals, int_mask=int_mask, steps=steps)


def reference(amplitudes, amp_mask, integrals, int_mask, steps):
    ladder = jnp.zeros((M, NB), jnp.float32)
    for step_index in range(STEPS):
        owner = steps[step_index].astype(jnp.int32)
        amp_panel = lax.dynamic_slice_in_dim(amplitudes, owner * KP, KP, 1).astype(jnp.float32)
        panel_mask = lax.dynamic_slice_in_dim(amp_mask, owner * PT, PT, 1).astype(jnp.float32)
        amp_panel = (amp_panel.reshape(M // TW, TW, PT, TW) * panel_mask[:, None, :, None]).reshape(M, KP)
        int_block = integrals[step_index].astype(jnp.float32)
        block_mask = int_mask[step_index].astype(jnp.float32)
        int_block = (int_block.reshape(PT, TW, NB // TW, TW) * block_mask[:, None, :, None]).reshape(KP, NB)
        ladder = ladder + jnp.dot(amp_panel, int_block, precision=lax.Precision.HIGHEST, preferred_element_type=jnp.float32)
    return ladder
```

```python
import jax
import jax.numpy as jnp
from jax import lax
from jax.experimental import pallas as pl
from jax.experimental.pallas import tpu as pltpu
from jax.sharding import Mesh
from jax.sharding import PartitionSpec as P

TW = 128
STEPS = 2
RING = 4
ROW = ("y", "core")
COL = ("z", "x")
GRID = ("core", "z", "x")


def plane_perm(first, shift):
    pairs = []
    for core in range(2):
        for z in range(RING):
            for x in range(RING):
                along_z = (core == 0) == first
                to_z, to_x = ((z + shift) % RING, x) if along_z else (z, (x + shift) % RING)
                pairs.append((core * 16 + z * RING + x, core * 16 + to_z * RING + to_x))
    return pairs


def wrap(value):
    return lax.rem(value + 2 * RING, RING)


def origin(core, z, x, first_shift, second_shift):
    on_zero = wrap(z - first_shift) * RING + wrap(x - second_shift)
    on_one = wrap(z - second_shift) * RING + wrap(x - first_shift)
    return jnp.where(core == 0, on_zero, on_one)


def needed_tile(mask_ref, group):
    found = mask_ref[0, 2 * group + 1]
    for row in range(1, 8):
        found = found | mask_ref[row, 2 * group + 1]
    return jnp.where(found != 0, 1, 0)


def compress_kernel(mask_ref, info_ref, *refs):
    tiles, out_ref = refs[:-1], refs[-1]
    width = len(tiles)
    for place, tile_ref in enumerate(tiles):
        group = pl.program_id(0) * width + place
        column = 2 * group + needed_tile(mask_ref, group)
        for row in range(8):
            keep = mask_ref[row, column] != 0
            rows = slice(row * TW, (row + 1) * TW)
            tile = tile_ref[rows, :]
            for step in range(STEPS):
                shown = keep & (info_ref[step] == info_ref[2])
                out_ref[step, rows, place * TW:(place + 1) * TW] = jnp.where(shown, tile, jnp.zeros_like(tile))


def compress(amplitudes, amp_mask, info):
    rows = amplitudes.shape[0]
    groups = amp_mask.shape[1] // 2
    width = 2

    def column(place):
        def index(step, mask_ref, info_ref):
            group = step * width + place
            return 0, 2 * group + needed_tile(mask_ref, group)
        return index

    return pl.pallas_call(
        compress_kernel,
        grid_spec=pltpu.PrefetchScalarGridSpec(
            num_scalar_prefetch=2,
            grid=(groups // width,),
            in_specs=[pl.BlockSpec((rows, TW), column(place)) for place in range(width)],
            out_specs=pl.BlockSpec((STEPS, rows, width * TW), lambda step, *_: (0, 0, step)),
        ),
        out_shape=jax.ShapeDtypeStruct((STEPS, rows, groups * TW), amplitudes.dtype),
        compiler_params=pltpu.CompilerParams(vmem_limit_bytes=32 << 20),
        name="compress",
    )(amp_mask, info, *([amplitudes] * width))


def pick_kernel(step, needs_ref, info_ref, *refs):
    held, sent, sems = refs[:RING], refs[RING:2 * RING], refs[2 * RING]
    core, z, x = info_ref[3], info_ref[4], info_ref[5]
    copies = []
    for second in range(RING):
        reader = origin(core, z, x, 0, -second)
        for first in range(RING):
            group = origin(core, z, x, first, 0)
            tile = needs_ref[reader, step * 16 + group]
            copies.append(pltpu.make_async_copy(
                held[first].at[tile], sent[second].at[first], sems.at[second * RING + first]))
            copies[-1].start()
    for copy in copies:
        copy.wait()


def pick(step, needs, info, held):
    shape = jax.ShapeDtypeStruct((RING,) + held[0].shape[1:], held[0].dtype)
    return pl.pallas_call(
        lambda *refs: pick_kernel(step, *refs),
        in_specs=[pl.BlockSpec(memory_space=pltpu.SMEM)] * 2 + [pl.BlockSpec(memory_space=pl.ANY)] * RING,
        out_specs=[pl.BlockSpec(memory_space=pl.ANY)] * RING,
        out_shape=[shape] * RING,
        scratch_shapes=[pltpu.SemaphoreType.DMA((RING * RING,))],
        name="pick",
    )(needs, info, *held)


def ladder_kernel(info_ref, panel_ref, *refs):
    blocks, out_ref, gathered, sems = refs[:-3], refs[-3], refs[-2], refs[-1]
    depth = panel_ref.shape[2]

    @pl.when(pl.program_id(0) == 0)
    def _():
        core, z, x = info_ref[3], info_ref[4], info_ref[5]
        copies = []
        for step in range(STEPS):
            for second in range(RING):
                for first in range(RING):
                    place = origin(core, z, x, first, second)
                    start = pl.multiple_of(step * depth + place * TW, TW)
                    copies.append(pltpu.make_async_copy(
                        blocks[step * RING + second].at[first],
                        gathered.at[pl.ds(start, TW), :],
                        sems.at[len(copies)]))
                    copies[-1].start()
        for copy in copies:
            copy.wait()

    total = jnp.dot(panel_ref[0], gathered[:depth, :], preferred_element_type=jnp.float32)
    total += jnp.dot(panel_ref[1], gathered[depth:, :], preferred_element_type=jnp.float32)
    out_ref[...] = total


def multiply(info, panels, blocks):
    steps, rows, depth = panels.shape
    width = blocks[0].shape[-1]
    part = 256
    return pl.pallas_call(
        ladder_kernel,
        grid=(rows // part,),
        in_specs=[pl.BlockSpec(memory_space=pltpu.SMEM),
                  pl.BlockSpec((steps, part, depth), lambda m: (0, m, 0))]
        + [pl.BlockSpec(memory_space=pl.ANY)] * len(blocks),
        out_specs=pl.BlockSpec((part, width), lambda m: (m, 0)),
        out_shape=jax.ShapeDtypeStruct((rows, width), jnp.float32),
        scratch_shapes=[pltpu.VMEM((steps * depth, width), panels.dtype),
                        pltpu.SemaphoreType.DMA((steps * RING * RING,))],
        compiler_params=pltpu.CompilerParams(vmem_limit_bytes=40 << 20),
        cost_estimate=pl.CostEstimate(flops=2 * rows * steps * depth * width, bytes_accessed=24 << 20, transcendentals=0),
        name="ladder",
    )(info, panels, *blocks)


def local(amplitudes, amp_mask, integrals, int_mask, steps):
    tiles, ab_width = integrals.shape[1] // TW, integrals.shape[2]
    row = lax.axis_index(ROW)
    core, z, x = (lax.axis_index(axis) for axis in GRID)
    info = jnp.stack([steps[0], steps[1], row, core, z, x]).astype(jnp.int32)

    panels = lax.psum(compress(amplitudes, amp_mask, info), ROW)

    held = []
    for step in range(STEPS):
        gate = int_mask[step].astype(integrals.dtype)[:, None, :, None]
        block = integrals[step].reshape(tiles, TW, ab_width // TW, TW) * gate
        block = block.reshape(tiles, TW, ab_width)
        held.append([block] + [lax.ppermute(block, GRID, plane_perm(True, shift)) for shift in (1, 3, 2)])
        held[-1] = [held[-1][i] for i in (0, 1, 3, 2)]

    own = jnp.max(amp_mask, axis=0).reshape(-1, 2)[:, 1]
    groups = own.shape[0]
    by_row = lax.all_to_all(jnp.broadcast_to(own, (8, groups)), ROW, 0, 0, tiled=True)
    chosen = jnp.sum(jnp.where((steps[:, None] == jnp.arange(8))[:, :, None], by_row[None], 0), axis=1)
    needs = lax.all_to_all(
        jnp.broadcast_to(chosen.reshape(1, -1), (16, STEPS * groups)), COL, 0, 0, tiled=True)

    blocks = []
    for step in range(STEPS):
        sent = pick(step, needs, info, held[step])
        here = [sent[0]] + [lax.ppermute(sent[shift], GRID, plane_perm(False, shift)) for shift in (1, 2, 3)]
        blocks.extend(here)
    return multiply(info, panels, blocks)


def solution(mesh):
    grid = Mesh(mesh.devices.reshape(4, 2, 4, 4), ("y", "core", "z", "x"))
    return jax.shard_map(
        local,
        mesh=grid,
        in_specs=(P(COL, ROW), P(COL, ROW), P(None, COL, ROW), P(None, COL, ROW), P()),
        out_specs=P(COL, ROW),
        check_vma=False,
    )
```

```python
import jax
import jax.numpy as jnp
from jax import lax
from jax.experimental import pallas as pl
from jax.experimental.pallas import tpu as pltpu
from jax.sharding import Mesh
from jax.sharding import PartitionSpec as P

TW = 128
STEPS = 2
RING = 4
ROW = ("y", "core")
COL = ("z", "x")
GRID = ("core", "z", "x")


def plane_perm(first, shift):
    pairs = []
    for core in range(2):
        for z in range(RING):
            for x in range(RING):
                along_z = (core == 0) == first
                to_z, to_x = ((z + shift) % RING, x) if along_z else (z, (x + shift) % RING)
                pairs.append((core * 16 + z * RING + x, core * 16 + to_z * RING + to_x))
    return pairs


def wrap(value):
    return lax.rem(value + 2 * RING, RING)


def origin(core, z, x, first_shift, second_shift):
    on_zero = wrap(z - first_shift) * RING + wrap(x - second_shift)
    on_one = wrap(z - second_shift) * RING + wrap(x - first_shift)
    return jnp.where(core == 0, on_zero, on_one)


def needed_tile(mask_ref, group):
    found = mask_ref[0, 2 * group + 1]
    for row in range(1, 8):
        found = found | mask_ref[row, 2 * group + 1]
    return jnp.where(found != 0, 1, 0)


def compress_kernel(mask_ref, info_ref, *refs):
    tiles, out_ref = refs[:-1], refs[-1]
    width = len(tiles)
    for place, tile_ref in enumerate(tiles):
        group = pl.program_id(0) * width + place
        column = 2 * group + needed_tile(mask_ref, group)
        for row in range(8):
            keep = mask_ref[row, column] != 0
            rows = slice(row * TW, (row + 1) * TW)
            tile = tile_ref[rows, :]
            for step in range(STEPS):
                shown = keep & (info_ref[step] == info_ref[2])
                out_ref[step, rows, place * TW:(place + 1) * TW] = jnp.where(shown, tile, jnp.zeros_like(tile))


def compress(amplitudes, amp_mask, info):
    rows = amplitudes.shape[0]
    groups = amp_mask.shape[1] // 2
    width = 2

    def column(place):
        def index(step, mask_ref, info_ref):
            group = step * width + place
            return 0, 2 * group + needed_tile(mask_ref, group)
        return index

    return pl.pallas_call(
        compress_kernel,
        grid_spec=pltpu.PrefetchScalarGridSpec(
            num_scalar_prefetch=2,
            grid=(groups // width,),
            in_specs=[pl.BlockSpec((rows, TW), column(place)) for place in range(width)],
            out_specs=pl.BlockSpec((STEPS, rows, width * TW), lambda step, *_: (0, 0, step)),
        ),
        out_shape=jax.ShapeDtypeStruct((STEPS, rows, groups * TW), amplitudes.dtype),
        compiler_params=pltpu.CompilerParams(vmem_limit_bytes=32 << 20),
        name="compress",
    )(amp_mask, info, *([amplitudes] * width))


def pick_kernel(step, needs_ref, info_ref, *refs):
    held, sent, sems = refs[:RING], refs[RING:2 * RING], refs[2 * RING]
    core, z, x = info_ref[3], info_ref[4], info_ref[5]
    copies = []
    for second in range(RING):
        reader = origin(core, z, x, 0, -second)
        for first in range(RING):
            group = origin(core, z, x, first, 0)
            tile = needs_ref[reader, step * 16 + group]
            copies.append(pltpu.make_async_copy(
                held[first].at[tile], sent[second].at[first], sems.at[second * RING + first]))
            copies[-1].start()
    for copy in copies:
        copy.wait()


def pick(step, needs, info, held):
    shape = jax.ShapeDtypeStruct((RING,) + held[0].shape[1:], held[0].dtype)
    return pl.pallas_call(
        lambda *refs: pick_kernel(step, *refs),
        in_specs=[pl.BlockSpec(memory_space=pltpu.SMEM)] * 2 + [pl.BlockSpec(memory_space=pltpu.VMEM)] * RING,
        out_specs=[pl.BlockSpec(memory_space=pl.ANY)] * RING,
        out_shape=[shape] * RING,
        scratch_shapes=[pltpu.SemaphoreType.DMA((RING * RING,))],
        name="pick",
    )(needs, info, *held)


def ladder_kernel(info_ref, panel_ref, *refs):
    blocks, out_ref = refs[:-1], refs[-1]
    core, z, x = info_ref[3], info_ref[4], info_ref[5]
    total = None
    for step in range(STEPS):
        for second in range(RING):
            columns = []
            for first in range(RING):
                start = pl.multiple_of(origin(core, z, x, first, second) * TW, TW)
                columns.append(panel_ref[step, :, pl.ds(start, TW)])
            block_ref = blocks[step * RING + second]
            block = block_ref[...].reshape(RING * TW, block_ref.shape[2])
            part = jnp.dot(jnp.concatenate(columns, axis=1), block, preferred_element_type=jnp.float32)
            total = part if total is None else total + part
    out_ref[...] = total


def multiply(info, panels, blocks):
    steps, rows, depth = panels.shape
    width = blocks[0].shape[-1]
    part = 256
    return pl.pallas_call(
        ladder_kernel,
        grid=(rows // part,),
        in_specs=[pl.BlockSpec(memory_space=pltpu.SMEM),
                  pl.BlockSpec((steps, part, depth), lambda m: (0, m, 0))]
        + [pl.BlockSpec(memory_space=pltpu.VMEM)] * len(blocks),
        out_specs=pl.BlockSpec((part, width), lambda m: (m, 0)),
        out_shape=jax.ShapeDtypeStruct((rows, width), jnp.float32),
        compiler_params=pltpu.CompilerParams(vmem_limit_bytes=40 << 20),
        cost_estimate=pl.CostEstimate(flops=2 * rows * steps * depth * width, bytes_accessed=24 << 20, transcendentals=0),
        name="ladder",
    )(info, panels, *blocks)


def local(amplitudes, amp_mask, integrals, int_mask, steps):
    tiles, ab_width = integrals.shape[1] // TW, integrals.shape[2]
    row = lax.axis_index(ROW)
    core, z, x = (lax.axis_index(axis) for axis in GRID)
    info = jnp.stack([steps[0], steps[1], row, core, z, x]).astype(jnp.int32)

    panels = lax.psum(compress(amplitudes, amp_mask, info), ROW)

    held = []
    for step in range(STEPS):
        gate = int_mask[step].astype(integrals.dtype)[:, None, :, None]
        block = integrals[step].reshape(tiles, TW, ab_width // TW, TW) * gate
        block = block.reshape(tiles, TW, ab_width)
        held.append([block] + [lax.ppermute(block, GRID, plane_perm(True, shift)) for shift in (1, 3, 2)])
        held[-1] = [held[-1][i] for i in (0, 1, 3, 2)]

    own = jnp.max(amp_mask, axis=0).reshape(-1, 2)[:, 1]
    groups = own.shape[0]
    by_row = lax.all_to_all(jnp.broadcast_to(own, (8, groups)), ROW, 0, 0, tiled=True)
    chosen = jnp.sum(jnp.where((steps[:, None] == jnp.arange(8))[:, :, None], by_row[None], 0), axis=1)
    needs = lax.all_to_all(
        jnp.broadcast_to(chosen.reshape(1, -1), (16, STEPS * groups)), COL, 0, 0, tiled=True)

    blocks = []
    for step in range(STEPS):
        sent = pick(step, needs, info, held[step])
        here = [sent[0]] + [lax.ppermute(sent[shift], GRID, plane_perm(False, shift)) for shift in (1, 2, 3)]
        blocks.extend(here)
    return multiply(info, panels, blocks)


def solution(mesh):
    grid = Mesh(mesh.devices.reshape(4, 2, 4, 4), ("y", "core", "z", "x"))
    return jax.shard_map(
        local,
        mesh=grid,
        in_specs=(P(COL, ROW), P(COL, ROW), P(None, COL, ROW), P(None, COL, ROW), P()),
        out_specs=P(COL, ROW),
        check_vma=False,
    )
```

```python
import functools

import jax
import jax.numpy as jnp
from jax import lax
from jax.experimental import pallas as pl
from jax.experimental.pallas import tpu as pltpu
from jax.sharding import Mesh
from jax.sharding import PartitionSpec as P

TW = 128
PART = 256
STEPS = 2
RING = 4
ROWS = 8
ROW = ("y", "core")
COL = ("z", "x")
GRID = ("core", "z", "x")


def plane_perm(first, shift):
    pairs = []
    for core in range(2):
        for z in range(RING):
            for x in range(RING):
                along_z = (core == 0) == first
                to_z, to_x = ((z + shift) % RING, x) if along_z else (z, (x + shift) % RING)
                pairs.append((core * 16 + z * RING + x, core * 16 + to_z * RING + to_x))
    return pairs


def wrap(value):
    return lax.rem(value + 2 * RING, RING)


def origin(core, z, x, first_shift, second_shift):
    on_zero = wrap(z - first_shift) * RING + wrap(x - second_shift)
    on_one = wrap(z - second_shift) * RING + wrap(x - first_shift)
    return jnp.where(core == 0, on_zero, on_one)


def needed_tile(mask_ref, group):
    found = mask_ref[0, 2 * group + 1]
    for row in range(1, 8):
        found = found | mask_ref[row, 2 * group + 1]
    return jnp.where(found != 0, 1, 0)


def compress_kernel(mask_ref, info_ref, after_ref, amp_ref, panel_ref, *refs):
    panels = [panel_ref.at[step] for step in range(STEPS)]
    (held, blank, in_sems, out_sems, blank_sems) = refs
    groups, rows, _ = held.shape
    row = info_ref[2]
    mine = [info_ref[step] == row for step in range(STEPS)]
    some = functools.reduce(jnp.logical_or, mine)
    loads, columns = [], []
    for group in range(groups):
        column = 2 * group + needed_tile(mask_ref, group)
        columns.append(column)
        loads.append(pltpu.make_async_copy(
            amp_ref.at[:, pl.ds(pl.multiple_of(column * TW, TW), TW)], held.at[group], in_sems.at[group]))

    @pl.when(some)
    def _():
        for load in loads:
            load.start()

    blank[...] = jnp.zeros_like(blank)
    for step in range(STEPS):
        @pl.when(jnp.logical_not(mine[step]))
        def _():
            for group in range(groups):
                pltpu.make_async_copy(blank, panels[step].at[group], blank_sems.at[step, group]).start()

    @pl.when(some)
    def _():
        for group, load in enumerate(loads):
            load.wait()
            for tile in range(rows // TW):
                span = slice(tile * TW, (tile + 1) * TW)

                @pl.when(mask_ref[tile, columns[group]] == 0)
                def _():
                    held[group, span, :] = jnp.zeros((TW, TW), held.dtype)
            for step in range(STEPS):
                @pl.when(mine[step])
                def _():
                    pltpu.make_async_copy(held.at[group], panels[step].at[group], out_sems.at[group]).start()
        for group in range(groups):
            pltpu.make_async_copy(held.at[group], panels[0].at[group], out_sems.at[group]).wait()

    for step in range(STEPS):
        @pl.when(jnp.logical_not(mine[step]))
        def _():
            for group in range(groups):
                pltpu.make_async_copy(blank, panels[step].at[group], blank_sems.at[step, group]).wait()


def compress(amplitudes, amp_mask, info, after):
    rows, groups = amplitudes.shape[0], amp_mask.shape[1] // 2
    return pl.pallas_call(
        compress_kernel,
        in_specs=[pl.BlockSpec(memory_space=pltpu.SMEM)] * 2 + [pl.BlockSpec(memory_space=pl.ANY)] * 2,
        out_specs=pl.BlockSpec(memory_space=pl.ANY),
        out_shape=jax.ShapeDtypeStruct((STEPS, groups, rows, TW), amplitudes.dtype),
        scratch_shapes=[pltpu.VMEM((groups, rows, TW), amplitudes.dtype),
                        pltpu.VMEM((rows, TW), amplitudes.dtype),
                        pltpu.SemaphoreType.DMA((groups,)), pltpu.SemaphoreType.DMA((groups,)),
                        pltpu.SemaphoreType.DMA((STEPS, groups))],
        compiler_params=pltpu.CompilerParams(vmem_limit_bytes=60 << 20),
        name="compress",
    )(amp_mask, info, after, amplitudes)


def pick_kernel(needs_ref, info_ref, *refs):
    held, sent, sems = refs[:RING], refs[RING:2 * RING - 1], refs[2 * RING - 1]
    core, z, x = info_ref[3], info_ref[4], info_ref[5]
    copies = []
    for second in range(1, RING):
        reader = origin(core, z, x, 0, -second)
        for step in range(STEPS):
            for first in range(RING):
                group = origin(core, z, x, first, 0)
                tile = needs_ref[reader, step * 16 + group]
                copies.append(pltpu.make_async_copy(
                    held[first].at[step, tile], sent[second - 1].at[step, first], sems.at[len(copies)]))
                copies[-1].start()
    for copy in copies:
        copy.wait()


def pick(needs, info, held):
    steps, _, rows, width = held[0].shape
    shape = jax.ShapeDtypeStruct((steps, RING, rows, width), held[0].dtype)
    return pl.pallas_call(
        pick_kernel,
        in_specs=[pl.BlockSpec(memory_space=pltpu.SMEM)] * 2 + [pl.BlockSpec(memory_space=pltpu.VMEM)] * RING,
        out_specs=[pl.BlockSpec(memory_space=pl.ANY)] * (RING - 1),
        out_shape=[shape] * (RING - 1),
        scratch_shapes=[pltpu.SemaphoreType.DMA((steps * (RING - 1) * RING,))],
        compiler_params=pltpu.CompilerParams(vmem_limit_bytes=8 << 20),
        name="pick",
    )(needs, info, *held)


def ladder_kernel(needs_ref, info_ref, panel_ref, *refs):
    held, blocks, (out_ref, lefts, rights, total, left_sems, right_sems, out_sems) = (
        refs[:RING], refs[RING:2 * RING - 1], refs[2 * RING - 1:])
    core, z, x = info_ref[3], info_ref[4], info_ref[5]
    me = z * RING + x
    parts = total.shape[0]
    rows = total.shape[1]
    loads = []
    for step in range(STEPS):
        for second in range(RING):
            slot = len(loads)
            loads.append([])
            for first in range(RING):
                if second == 0:
                    tile = needs_ref[me, step * 16 + origin(core, z, x, first, 0)]
                    source = held[first].at[step, tile]
                else:
                    source = blocks[second - 1].at[step, first]
                group = origin(core, z, x, first, second)
                loads[slot].append(pltpu.make_async_copy(
                    panel_ref.at[step, group], lefts.at[step, :, pl.ds((second * RING + first) * TW, TW)], left_sems.at[slot, first]))
                loads[slot].append(pltpu.make_async_copy(
                    source, rights.at[step, pl.ds((second * RING + first) * TW, TW)], right_sems.at[slot, first]))
            for load in loads[slot]:
                load.start()
    for start, stop in ((0, 1), (1, RING), (RING, STEPS * RING)):
        for slot_loads in loads[start:stop]:
            for load in slot_loads:
                load.wait()

        @pl.loop(0, parts)
        def _(part):
            span = pl.ds(pl.multiple_of(part * PART, PART), PART)
            step, skip = start // RING, start % RING
            depth = slice(skip * RING * TW, (skip + stop - start) * RING * TW)
            product = jnp.dot(lefts[step, :, depth], rights[step, depth, span], preferred_element_type=jnp.float32)
            total[part] = product if start == 0 else total[part] + product
            if stop == len(loads):
                pltpu.make_async_copy(total.at[part], out_ref.at[:, span], out_sems.at[part]).start()

    for part in range(parts):
        pltpu.make_async_copy(total.at[part], out_ref.at[:, pl.ds(part * PART, PART)], out_sems.at[part]).wait()


def multiply(needs, info, panels, held, blocks):
    steps, groups, rows, _ = panels.shape
    depth, width = groups * TW, held[0].shape[-1]
    slots = steps * RING
    return pl.pallas_call(
        ladder_kernel,
        in_specs=[pl.BlockSpec(memory_space=pltpu.SMEM)] * 2 + [pl.BlockSpec(memory_space=pl.ANY)] * (2 * RING),
        out_specs=pl.BlockSpec(memory_space=pl.ANY),
        out_shape=jax.ShapeDtypeStruct((rows, width), jnp.float32),
        scratch_shapes=[pltpu.VMEM((steps, rows, groups * TW), panels.dtype),
                        pltpu.VMEM((steps, groups * TW, width), panels.dtype),
                        pltpu.VMEM((width // PART, rows, PART), jnp.float32),
                        pltpu.SemaphoreType.DMA((slots, RING)),
                        pltpu.SemaphoreType.DMA((slots, RING)),
                        pltpu.SemaphoreType.DMA((width // PART,))],
        compiler_params=pltpu.CompilerParams(vmem_limit_bytes=60 << 20),
        cost_estimate=pl.CostEstimate(flops=2 * rows * steps * depth * width, bytes_accessed=24 << 20, transcendentals=0),
        name="ladder",
    )(needs, info, panels, *held, *blocks)


def local(amplitudes, amp_mask, integrals, int_mask, steps):
    tiles, ab_width = integrals.shape[1] // TW, integrals.shape[2]
    row = lax.axis_index(ROW)
    core, z, x = (lax.axis_index(axis) for axis in GRID)
    info = jnp.stack([steps[0], steps[1], row, core, z, x]).astype(jnp.int32)

    gate = int_mask.astype(integrals.dtype)[:, :, None, :, None]
    block = integrals.reshape(STEPS, tiles, TW, ab_width // TW, TW) * gate
    block = block.reshape(STEPS, tiles, TW, ab_width)
    held = [block] + [lax.ppermute(block, GRID, plane_perm(True, shift)) for shift in (1, 2, 3)]

    panels = lax.psum(compress(amplitudes, amp_mask, info, block), ROW)

    own = jnp.max(amp_mask, axis=0).reshape(-1, 2)[:, 1]
    groups = own.shape[0]
    by_row = lax.all_to_all(jnp.broadcast_to(own, (8, groups)), ROW, 0, 0, tiled=True)
    chosen = jnp.sum(jnp.where((steps[:, None] == jnp.arange(8))[:, :, None], by_row[None], 0), axis=1)
    needs = lax.all_to_all(
        jnp.broadcast_to(chosen.reshape(1, -1), (16, STEPS * groups)), COL, 0, 0, tiled=True)

    sent = pick(needs, info, held)
    blocks = [lax.ppermute(sent[shift - 1], GRID, plane_perm(False, shift)) for shift in (1, 2, 3)]
    return multiply(needs, info, panels, held, blocks)


def solution(mesh):
    grid = Mesh(mesh.devices.reshape(4, 2, 4, 4), ("y", "core", "z", "x"))
    return jax.shard_map(
        local,
        mesh=grid,
        in_specs=(P(COL, ROW), P(COL, ROW), P(None, COL, ROW), P(None, COL, ROW), P()),
        out_specs=P(COL, ROW),
        check_vma=False,
    )
```

```python
import functools

import jax
import jax.numpy as jnp
from jax import lax
from jax.experimental import pallas as pl
from jax.experimental.pallas import tpu as pltpu
from jax.sharding import Mesh
from jax.sharding import PartitionSpec as P

TW = 128
PART = 256
STEPS = 2
RING = 4
ROWS = 8
ROW = ("y", "core")
COL = ("z", "x")
GRID = ("core", "z", "x")


def plane_perm(first, shift):
    pairs = []
    for core in range(2):
        for z in range(RING):
            for x in range(RING):
                along_z = (core == 0) == first
                to_z, to_x = ((z + shift) % RING, x) if along_z else (z, (x + shift) % RING)
                pairs.append((core * 16 + z * RING + x, core * 16 + to_z * RING + to_x))
    return pairs


def round_y(shift):
    return [(chip, (chip + shift) % RING) for chip in range(RING)]


def wrap(value):
    return value & (RING - 1)


def origin(core, z, x, first_shift, second_shift):
    on_zero = wrap(z - first_shift) * RING + wrap(x - second_shift)
    on_one = wrap(z - second_shift) * RING + wrap(x - first_shift)
    return jnp.where(core == 0, on_zero, on_one)


def needed_tile(mask_ref, group):
    found = mask_ref[0, 2 * group + 1]
    for row in range(1, 8):
        found = found | mask_ref[row, 2 * group + 1]
    return jnp.where(found != 0, 1, 0)


def column_loads(mask_ref, amp_ref, held, sems, groups):
    loads, columns = [], []
    for place, group in enumerate(groups):
        column = 2 * group + needed_tile(mask_ref, group)
        columns.append(column)
        loads.append(pltpu.make_async_copy(
            amp_ref.at[:, pl.ds(pl.multiple_of(column * TW, TW), TW)], held.at[place], sems.at[place]))
        loads[place].start()
    return loads, columns


def apply_mask(mask_ref, held, place, column):
    for tile in range(held.shape[1] // TW):
        span = slice(tile * TW, (tile + 1) * TW)

        @pl.when(mask_ref[tile, column] == 0)
        def _():
            held[place, span, :] = jnp.zeros((TW, TW), held.dtype)


def compress_kernel(mask_ref, amp_ref, out_ref, held, in_sems, out_sems):
    groups = held.shape[0]
    loads, columns = column_loads(mask_ref, amp_ref, held, in_sems, range(groups))
    stores = []
    for group, load in enumerate(loads):
        load.wait()
        apply_mask(mask_ref, held, group, columns[group])
        stores.append(pltpu.make_async_copy(held.at[group], out_ref.at[group], out_sems.at[group]))
        stores[-1].start()
    for store in stores:
        store.wait()


def compress(amplitudes, amp_mask):
    rows, groups = amplitudes.shape[0], amp_mask.shape[1] // 2
    kind = amplitudes.dtype
    return pl.pallas_call(
        compress_kernel,
        in_specs=[pl.BlockSpec(memory_space=pltpu.SMEM), pl.BlockSpec(memory_space=pl.ANY)],
        out_specs=pl.BlockSpec(memory_space=pl.ANY),
        out_shape=jax.ShapeDtypeStruct((groups, rows, TW), kind),
        scratch_shapes=[pltpu.VMEM((groups, rows, TW), kind),
                        pltpu.SemaphoreType.DMA((groups,)), pltpu.SemaphoreType.DMA((groups,))],
        compiler_params=pltpu.CompilerParams(vmem_limit_bytes=60 << 20),
        name="compress",
    )(amp_mask, amplitudes)


def choose_kernel(info_ref, after_ref, pieces_ref, out_ref, held, in_sems, out_sems):
    each = held.shape[1]
    loads = [pltpu.make_async_copy(pieces_ref.at[pl.ds(info_ref[step] * each, each)], held.at[step], in_sems.at[step])
             for step in range(STEPS)]
    stores = [pltpu.make_async_copy(held.at[step], out_ref.at[step], out_sems.at[step]) for step in range(STEPS)]
    for load in loads:
        load.start()
    for load, store in zip(loads, stores):
        load.wait()
        store.start()
    for store in stores:
        store.wait()


def choose(info, after, pieces):
    groups, rows, _ = pieces.shape
    shape = (STEPS, groups // ROWS, rows, TW)
    return pl.pallas_call(
        choose_kernel,
        in_specs=[pl.BlockSpec(memory_space=pltpu.SMEM)] + [pl.BlockSpec(memory_space=pl.ANY)] * 2,
        out_specs=pl.BlockSpec(memory_space=pl.ANY),
        out_shape=jax.ShapeDtypeStruct(shape, pieces.dtype),
        scratch_shapes=[pltpu.VMEM(shape, pieces.dtype),
                        pltpu.SemaphoreType.DMA((STEPS,)), pltpu.SemaphoreType.DMA((STEPS,))],
        compiler_params=pltpu.CompilerParams(vmem_limit_bytes=4 << 20),
        name="choose",
    )(info, after, pieces)


def pick_kernel(needs_ref, info_ref, *refs):
    held, sent, sems = refs[:RING], refs[RING:2 * RING - 1], refs[2 * RING - 1]
    core, z, x = info_ref[3], info_ref[4], info_ref[5]
    copies = []
    for second in range(1, RING):
        for step in range(STEPS):
            for first in range(RING):
                group = origin(core, z, x, first, 0)
                tile = needs_ref[info_ref[step], second * 16 + group]
                copies.append(pltpu.make_async_copy(
                    held[first].at[step, tile], sent[second - 1].at[step, first], sems.at[len(copies)]))
                copies[-1].start()
    for copy in copies:
        copy.wait()


def pick(needs, info, held):
    steps, _, rows, width = held[0].shape
    shape = jax.ShapeDtypeStruct((steps, RING, rows, width), held[0].dtype)
    return pl.pallas_call(
        pick_kernel,
        in_specs=[pl.BlockSpec(memory_space=pltpu.SMEM)] * 2 + [pl.BlockSpec(memory_space=pltpu.VMEM)] * RING,
        out_specs=[pl.BlockSpec(memory_space=pl.ANY)] * (RING - 1),
        out_shape=[shape] * (RING - 1),
        scratch_shapes=[pltpu.SemaphoreType.DMA((steps * (RING - 1) * RING,))],
        compiler_params=pltpu.CompilerParams(vmem_limit_bytes=8 << 20),
        cost_estimate=pl.CostEstimate(flops=18400000000, bytes_accessed=8 << 20, transcendentals=0),
        name="pick",
    )(needs, info, *held)


def ladder_kernel(needs_ref, info_ref, *refs):
    halves, refs = refs[:10], refs[10:]
    held, blocks, (out_ref, lefts, rights, total, left_sems, right_sems, out_sems) = (
        refs[:RING], refs[RING:2 * RING - 1], refs[2 * RING - 1:])
    chip, core, z, x = (info_ref[2] >> 1), info_ref[3], info_ref[4], info_ref[5]
    each = halves[0].shape[1]
    parts = total.shape[0]

    def left(source, step, group):
        start = pl.multiple_of(group * TW, TW)
        return pltpu.make_async_copy(source, lefts.at[step, :, pl.ds(start, TW)], left_sems.at[step, group])

    def slot_of(group):
        back_z, back_x = wrap(z - (group >> 2)), wrap(x - group)
        return jnp.where(core == 0, back_x * RING + back_z, back_z * RING + back_x)

    def right(source, step, second, first=0, count=RING):
        return pltpu.make_async_copy(
            source, rights.at[step, pl.ds((second * RING + first) * TW, count * TW)], right_sems.at[step, second])

    def block(step, second):
        return blocks[second - 1].at[step]

    for step in range(STEPS):
        for place, half in enumerate((core, 1 - core)):
            for shift in range(RING):
                for inner in range(each):
                    group = (wrap(chip - shift) * 2 + half) * each + inner
                    part = halves[place * 5 + (0, 1, 3 + step, 2)[shift]]
                    left(part.at[inner] if shift == 2 else part.at[step, inner], step, slot_of(group)).start()
        for first in range(RING):
            tile = needs_ref[info_ref[step], origin(core, z, x, first, 0)]
            right(held[first].at[step, tile], step, 0, first, 1).start()
        for second in range(1, RING):
            right(block(step, second), step, second).start()

    for step, start, stop in ((0, 0, 1), (0, 1, RING), (1, 0, RING)):
        for second in range(start, stop):
            for first in range(RING):
                left(halves[0].at[step, 0], step, second * RING + first).wait()
            right(block(step, 1), step, second).wait()

        @pl.loop(0, parts)
        def _(part):
            span = pl.ds(pl.multiple_of(part * PART, PART), PART)
            depth = slice(start * RING * TW, stop * RING * TW)
            product = jnp.dot(lefts[step, :, depth], rights[step, depth, span], preferred_element_type=jnp.float32)
            total[part] = product if step == 0 and start == 0 else total[part] + product
            if step == STEPS - 1:
                pltpu.make_async_copy(total.at[part], out_ref.at[:, span], out_sems.at[part]).start()

    for part in range(parts):
        pltpu.make_async_copy(total.at[part], out_ref.at[:, pl.ds(part * PART, PART)], out_sems.at[part]).wait()


def multiply(needs, info, halves, held, blocks):
    steps, each, rows, _ = halves[0].shape
    groups = 2 * RING * each
    depth, width = groups * TW, held[0].shape[-1]
    kind = held[0].dtype
    return pl.pallas_call(
        ladder_kernel,
        in_specs=[pl.BlockSpec(memory_space=pltpu.SMEM)] * 2
        + [pl.BlockSpec(memory_space=pl.ANY)] * (len(halves) + len(held) + len(blocks)),
        out_specs=pl.BlockSpec(memory_space=pl.ANY),
        out_shape=jax.ShapeDtypeStruct((rows, width), jnp.float32),
        scratch_shapes=[pltpu.VMEM((steps, rows, depth), kind),
                        pltpu.VMEM((steps, depth, width), kind),
                        pltpu.VMEM((width // PART, rows, PART), jnp.float32),
                        pltpu.SemaphoreType.DMA((steps, groups)),
                        pltpu.SemaphoreType.DMA((steps, RING)),
                        pltpu.SemaphoreType.DMA((width // PART,))],
        compiler_params=pltpu.CompilerParams(vmem_limit_bytes=60 << 20),
        cost_estimate=pl.CostEstimate(flops=2 * rows * steps * depth * width, bytes_accessed=24 << 20, transcendentals=0),
        name="ladder",
    )(needs, info, *halves, *held, *[block.reshape(steps, RING * TW, width) for block in blocks])


def local(amplitudes, amp_mask, integrals, int_mask, steps):
    tiles, ab_width = integrals.shape[1] // TW, integrals.shape[2]
    row = lax.axis_index(ROW)
    core, z, x = (lax.axis_index(axis) for axis in GRID)
    info = jnp.stack([steps[0], steps[1], row, core, z, x]).astype(jnp.int32)

    own = jnp.max(amp_mask, axis=0).reshape(1, -1, 2)[:, :, 1]
    by_row = lax.all_to_all(jnp.broadcast_to(own, (ROWS, own.shape[1])), ROW, 0, 0, tiled=True)
    readers = [by_row] + [lax.ppermute(by_row, GRID, plane_perm(False, RING - ahead)) for ahead in (1, 2, 3)]
    needs = jnp.concatenate(readers, axis=1)

    gate = int_mask.astype(integrals.dtype)[:, :, None, :, None]
    block = integrals.reshape(STEPS, tiles, TW, ab_width // TW, TW) * gate
    block = block.reshape(STEPS, tiles, TW, ab_width)
    held = [block] + [lax.ppermute(block, GRID, plane_perm(True, shift)) for shift in (1, 2, 3)]

    sent = pick(needs, info, held)
    pieces = lax.all_to_all(compress(amplitudes, amp_mask), ROW, 0, 0, tiled=True)
    halves = [choose(info, sent[0], pieces)]
    halves += [lax.ppermute(halves[0], "y", round_y(shift)) for shift in (1, 3)]
    halves += [lax.ppermute(halves[1][0], "y", round_y(1)), lax.ppermute(halves[2][1], "y", round_y(3))]
    halves += [lax.ppermute(half, "core", [(0, 1), (1, 0)]) for half in halves]

    blocks = [lax.ppermute(sent[shift - 1], GRID, plane_perm(False, shift)) for shift in (1, 2, 3)]
    return multiply(needs, info, halves, held, blocks)


def solution(mesh):
    grid = Mesh(mesh.devices.reshape(4, 2, 4, 4), ("y", "core", "z", "x"))
    return jax.shard_map(
        local,
        mesh=grid,
        in_specs=(P(COL, ROW), P(COL, ROW), P(None, COL, ROW), P(None, COL, ROW), P()),
        out_specs=P(COL, ROW),
        check_vma=False,
    )
```

```python
import functools

import jax
import jax.numpy as jnp
from jax import lax
from jax.experimental import pallas as pl
from jax.experimental.pallas import tpu as pltpu
from jax.sharding import Mesh
from jax.sharding import PartitionSpec as P

TW = 128
PART = 256
STEPS = 2
RING = 4
ROWS = 8
ROW = ("y", "core")
COL = ("z", "x")
GRID = ("core", "z", "x")


def plane_perm(first, shift):
    pairs = []
    for core in range(2):
        for z in range(RING):
            for x in range(RING):
                along_z = (core == 0) == first
                to_z, to_x = ((z + shift) % RING, x) if along_z else (z, (x + shift) % RING)
                pairs.append((core * 16 + z * RING + x, core * 16 + to_z * RING + to_x))
    return pairs


def round_y(shift):
    return [(chip, (chip + shift) % RING) for chip in range(RING)]


def wrap(value):
    return value & (RING - 1)


def origin(core, z, x, first_shift, second_shift):
    on_zero = wrap(z - first_shift) * RING + wrap(x - second_shift)
    on_one = wrap(z - second_shift) * RING + wrap(x - first_shift)
    return jnp.where(core == 0, on_zero, on_one)


def needed_tile(mask_ref, group):
    found = mask_ref[0, 2 * group + 1]
    for row in range(1, 8):
        found = found | mask_ref[row, 2 * group + 1]
    return jnp.where(found != 0, 1, 0)


def column_loads(mask_ref, amp_ref, held, sems, groups):
    loads, columns = [], []
    for place, group in enumerate(groups):
        column = 2 * group + needed_tile(mask_ref, group)
        columns.append(column)
        loads.append(pltpu.make_async_copy(
            amp_ref.at[:, pl.ds(pl.multiple_of(column * TW, TW), TW)], held.at[place], sems.at[place]))
        loads[place].start()
    return loads, columns


def apply_mask(mask_ref, held, place, column):
    for tile in range(held.shape[1] // TW):
        span = slice(tile * TW, (tile + 1) * TW)

        @pl.when(mask_ref[tile, column] == 0)
        def _():
            held[place, span, :] = jnp.zeros((TW, TW), held.dtype)


def compress_kernel(mask_ref, amp_ref, out_ref, held, in_sems, out_sems):
    groups = held.shape[0]
    loads, columns = column_loads(mask_ref, amp_ref, held, in_sems, range(groups))
    stores = []
    for group, load in enumerate(loads):
        load.wait()
        apply_mask(mask_ref, held, group, columns[group])
        stores.append(pltpu.make_async_copy(held.at[group], out_ref.at[group], out_sems.at[group]))
        stores[-1].start()
    for store in stores:
        store.wait()


def compress(amplitudes, amp_mask):
    rows, groups = amplitudes.shape[0], amp_mask.shape[1] // 2
    kind = amplitudes.dtype
    return pl.pallas_call(
        compress_kernel,
        in_specs=[pl.BlockSpec(memory_space=pltpu.SMEM), pl.BlockSpec(memory_space=pl.ANY)],
        out_specs=pl.BlockSpec(memory_space=pl.ANY),
        out_shape=jax.ShapeDtypeStruct((groups, rows, TW), kind),
        scratch_shapes=[pltpu.VMEM((groups, rows, TW), kind),
                        pltpu.SemaphoreType.DMA((groups,)), pltpu.SemaphoreType.DMA((groups,))],
        compiler_params=pltpu.CompilerParams(vmem_limit_bytes=54 << 20),
        name="compress",
    )(amp_mask, amplitudes)


def choose_kernel(info_ref, after_ref, pieces_ref, out_ref, held, in_sems, out_sems):
    each = held.shape[1]
    loads = [pltpu.make_async_copy(pieces_ref.at[pl.ds(info_ref[step] * each, each)], held.at[step], in_sems.at[step])
             for step in range(STEPS)]
    stores = [pltpu.make_async_copy(held.at[step], out_ref.at[step], out_sems.at[step]) for step in range(STEPS)]
    for load in loads:
        load.start()
    for load, store in zip(loads, stores):
        load.wait()
        store.start()
    for store in stores:
        store.wait()


def choose(info, after, pieces):
    groups, rows, _ = pieces.shape
    shape = (STEPS, groups // ROWS, rows, TW)
    return pl.pallas_call(
        choose_kernel,
        in_specs=[pl.BlockSpec(memory_space=pltpu.SMEM)] + [pl.BlockSpec(memory_space=pl.ANY)] * 2,
        out_specs=pl.BlockSpec(memory_space=pl.ANY),
        out_shape=jax.ShapeDtypeStruct(shape, pieces.dtype),
        scratch_shapes=[pltpu.VMEM(shape, pieces.dtype),
                        pltpu.SemaphoreType.DMA((STEPS,)), pltpu.SemaphoreType.DMA((STEPS,))],
        compiler_params=pltpu.CompilerParams(vmem_limit_bytes=4 << 20),
        cost_estimate=pl.CostEstimate(flops=13800000000, bytes_accessed=2 << 20, transcendentals=0),
        name="choose",
    )(info, after, pieces)


def pick_kernel(needs_ref, info_ref, *refs):
    held, sent, sems = refs[:RING], refs[RING:2 * RING - 1], refs[2 * RING - 1]
    core, z, x = info_ref[3], info_ref[4], info_ref[5]
    copies = []
    for second in range(1, RING):
        for step in range(STEPS):
            for first in range(RING):
                group = origin(core, z, x, first, 0)
                tile = needs_ref[info_ref[step], second * 16 + group]
                copies.append(pltpu.make_async_copy(
                    held[first].at[step, tile], sent[second - 1].at[step, first], sems.at[len(copies)]))
                copies[-1].start()
    for copy in copies:
        copy.wait()


def pick(needs, info, held):
    steps, _, rows, width = held[0].shape
    shape = jax.ShapeDtypeStruct((steps, RING, rows, width), held[0].dtype)
    return pl.pallas_call(
        pick_kernel,
        in_specs=[pl.BlockSpec(memory_space=pltpu.SMEM)] * 2 + [pl.BlockSpec(memory_space=pltpu.VMEM)] * RING,
        out_specs=[pl.BlockSpec(memory_space=pl.ANY)] * (RING - 1),
        out_shape=[shape] * (RING - 1),
        scratch_shapes=[pltpu.SemaphoreType.DMA((steps * (RING - 1) * RING,))],
        compiler_params=pltpu.CompilerParams(vmem_limit_bytes=8 << 20),
        cost_estimate=pl.CostEstimate(flops=27600000000, bytes_accessed=8 << 20, transcendentals=0),
        name="pick",
    )(needs, info, *held)


def ladder_kernel(needs_ref, info_ref, *refs):
    halves, refs = refs[:10], refs[10:]
    held, blocks, (out_ref, lefts, rights, total, left_sems, right_sems, out_sems) = (
        refs[:RING], refs[RING:2 * RING - 1], refs[2 * RING - 1:])
    chip, core, z, x = (info_ref[2] >> 1), info_ref[3], info_ref[4], info_ref[5]
    each = halves[0].shape[1]
    parts = total.shape[0]

    def left(source, step, group):
        start = pl.multiple_of(group * TW, TW)
        return pltpu.make_async_copy(source, lefts.at[step, :, pl.ds(start, TW)], left_sems.at[step, group])

    def slot_of(group):
        back_z, back_x = wrap(z - (group >> 2)), wrap(x - group)
        return jnp.where(core == 0, back_x * RING + back_z, back_z * RING + back_x)

    def right(source, step, second, first=0, count=RING):
        return pltpu.make_async_copy(
            source, rights.at[step, pl.ds((second * RING + first) * TW, count * TW)], right_sems.at[step, second])

    def block(step, second):
        return blocks[second - 1].at[step]

    for step in range(STEPS):
        for place, half in enumerate((core, 1 - core)):
            for shift in range(RING):
                for inner in range(each):
                    group = (wrap(chip - shift) * 2 + half) * each + inner
                    part = halves[place * 5 + (0, 1, 3 + step, 2)[shift]]
                    left(part.at[inner] if shift == 2 else part.at[step, inner], step, slot_of(group)).start()
        for first in range(RING):
            tile = needs_ref[info_ref[step], origin(core, z, x, first, 0)]
            right(held[first].at[step, tile], step, 0, first, 1).start()
        for second in range(1, RING):
            right(block(step, second), step, second).start()

    for step, start, stop in ((0, 0, RING), (1, 0, RING)):
        for second in range(start, stop):
            for first in range(RING):
                left(halves[0].at[step, 0], step, second * RING + first).wait()
            right(block(step, 1), step, second).wait()

        @pl.loop(0, parts)
        def _(part):
            span = pl.ds(pl.multiple_of(part * PART, PART), PART)
            depth = slice(start * RING * TW, stop * RING * TW)
            product = jnp.dot(lefts[step, :, depth], rights[step, depth, span], preferred_element_type=jnp.float32)
            total[part] = product if step == 0 and start == 0 else total[part] + product
            if step == STEPS - 1:
                pltpu.make_async_copy(total.at[part], out_ref.at[:, span], out_sems.at[part]).start()

    for part in range(parts):
        pltpu.make_async_copy(total.at[part], out_ref.at[:, pl.ds(part * PART, PART)], out_sems.at[part]).wait()


def multiply(needs, info, halves, held, blocks):
    steps, each, rows, _ = halves[0].shape
    groups = 2 * RING * each
    depth, width = groups * TW, held[0].shape[-1]
    kind = held[0].dtype
    return pl.pallas_call(
        ladder_kernel,
        in_specs=[pl.BlockSpec(memory_space=pltpu.SMEM)] * 2
        + [pl.BlockSpec(memory_space=pl.ANY)] * (len(halves) + len(held) + len(blocks)),
        out_specs=pl.BlockSpec(memory_space=pl.ANY),
        out_shape=jax.ShapeDtypeStruct((rows, width), jnp.float32),
        scratch_shapes=[pltpu.VMEM((steps, rows, depth), kind),
                        pltpu.VMEM((steps, depth, width), kind),
                        pltpu.VMEM((width // PART, rows, PART), jnp.float32),
                        pltpu.SemaphoreType.DMA((steps, groups)),
                        pltpu.SemaphoreType.DMA((steps, RING)),
                        pltpu.SemaphoreType.DMA((width // PART,))],
        compiler_params=pltpu.CompilerParams(vmem_limit_bytes=28 << 20),
        cost_estimate=pl.CostEstimate(flops=2 * rows * steps * depth * width, bytes_accessed=24 << 20, transcendentals=0),
        name="ladder",
    )(needs, info, *halves, *held, *[block.reshape(steps, RING * TW, width) for block in blocks])


def local(amplitudes, amp_mask, integrals, int_mask, steps):
    tiles, ab_width = integrals.shape[1] // TW, integrals.shape[2]
    row = lax.axis_index(ROW)
    core, z, x = (lax.axis_index(axis) for axis in GRID)
    info = jnp.stack([steps[0], steps[1], row, core, z, x]).astype(jnp.int32)

    own = jnp.max(amp_mask, axis=0).reshape(1, -1, 2)[:, :, 1]
    by_row = lax.all_to_all(jnp.broadcast_to(own, (ROWS, own.shape[1])), ROW, 0, 0, tiled=True)
    readers = [by_row] + [lax.ppermute(by_row, GRID, plane_perm(False, RING - ahead)) for ahead in (1, 2, 3)]
    needs = jnp.concatenate(readers, axis=1)

    gate = int_mask.astype(integrals.dtype)[:, :, None, :, None]
    block = integrals.reshape(STEPS, tiles, TW, ab_width // TW, TW) * gate
    block = block.reshape(STEPS, tiles, TW, ab_width)
    held = [block] + [lax.ppermute(block, GRID, plane_perm(True, shift)) for shift in (1, 2, 3)]

    sent = pick(needs, info, held)
    pieces = lax.all_to_all(compress(amplitudes, amp_mask), ROW, 0, 0, tiled=True)
    halves = [choose(info, sent[0], pieces)]
    halves += [lax.ppermute(halves[0], "y", round_y(shift)) for shift in (1, 3)]
    halves += [lax.ppermute(halves[1][0], "y", round_y(1)), lax.ppermute(halves[2][1], "y", round_y(3))]
    halves += [lax.ppermute(half, "core", [(0, 1), (1, 0)]) for half in halves]

    blocks = [lax.ppermute(sent[shift - 1], GRID, plane_perm(False, shift)) for shift in (1, 2, 3)]
    return multiply(needs, info, halves, held, blocks)


def solution(mesh):
    grid = Mesh(mesh.devices.reshape(4, 2, 4, 4), ("y", "core", "z", "x"))
    return jax.shard_map(
        local,
        mesh=grid,
        in_specs=(P(COL, ROW), P(COL, ROW), P(None, COL, ROW), P(None, COL, ROW), P()),
        out_specs=P(COL, ROW),
        check_vma=False,
    )
```

```python
import functools

import jax
import jax.numpy as jnp
from jax import lax
from jax.experimental import pallas as pl
from jax.experimental.pallas import tpu as pltpu
from jax.sharding import Mesh
from jax.sharding import PartitionSpec as P

TW = 128
PART = 256
STEPS = 2
RING = 4
ROWS = 8
ROW = ("y", "core")
COL = ("z", "x")
GRID = ("core", "z", "x")


def plane_perm(first, shift):
    pairs = []
    for core in range(2):
        for z in range(RING):
            for x in range(RING):
                along_z = (core == 0) == first
                to_z, to_x = ((z + shift) % RING, x) if along_z else (z, (x + shift) % RING)
                pairs.append((core * 16 + z * RING + x, core * 16 + to_z * RING + to_x))
    return pairs


def round_y(shift):
    return [(chip, (chip + shift) % RING) for chip in range(RING)]


def wrap(value):
    return value & (RING - 1)


def origin(core, z, x, first_shift, second_shift):
    on_zero = wrap(z - first_shift) * RING + wrap(x - second_shift)
    on_one = wrap(z - second_shift) * RING + wrap(x - first_shift)
    return jnp.where(core == 0, on_zero, on_one)


def needed_tile(mask_ref, group):
    found = mask_ref[0, 2 * group + 1]
    for row in range(1, 8):
        found = found | mask_ref[row, 2 * group + 1]
    return jnp.where(found != 0, 1, 0)


def column_loads(mask_ref, amp_ref, held, sems, groups):
    loads, columns = [], []
    for place, group in enumerate(groups):
        column = 2 * group + needed_tile(mask_ref, group)
        columns.append(column)
        loads.append(pltpu.make_async_copy(
            amp_ref.at[:, pl.ds(pl.multiple_of(column * TW, TW), TW)], held.at[place], sems.at[place]))
        loads[place].start()
    return loads, columns


def apply_mask(mask_ref, held, place, column):
    for tile in range(held.shape[1] // TW):
        span = slice(tile * TW, (tile + 1) * TW)

        @pl.when(mask_ref[tile, column] == 0)
        def _():
            held[place, span, :] = jnp.zeros((TW, TW), held.dtype)


def compress_kernel(mask_ref, amp_ref, out_ref, held, in_sems, out_sems):
    groups = held.shape[0]
    loads, columns = column_loads(mask_ref, amp_ref, held, in_sems, range(groups))
    stores = []
    for group, load in enumerate(loads):
        load.wait()
        apply_mask(mask_ref, held, group, columns[group])
        stores.append(pltpu.make_async_copy(held.at[group], out_ref.at[group], out_sems.at[group]))
        stores[-1].start()
    for store in stores:
        store.wait()


def compress(amplitudes, amp_mask):
    rows, groups = amplitudes.shape[0], amp_mask.shape[1] // 2
    kind = amplitudes.dtype
    return pl.pallas_call(
        compress_kernel,
        in_specs=[pl.BlockSpec(memory_space=pltpu.SMEM), pl.BlockSpec(memory_space=pl.ANY)],
        out_specs=pl.BlockSpec(memory_space=pl.ANY),
        out_shape=jax.ShapeDtypeStruct((groups, rows, TW), kind),
        scratch_shapes=[pltpu.VMEM((groups, rows, TW), kind),
                        pltpu.SemaphoreType.DMA((groups,)), pltpu.SemaphoreType.DMA((groups,))],
        compiler_params=pltpu.CompilerParams(vmem_limit_bytes=54 << 20),
        name="compress",
    )(amp_mask, amplitudes)


def pick_kernel(needs_ref, info_ref, *refs):
    held, sent, sems = refs[:RING], refs[RING:2 * RING - 1], refs[2 * RING - 1]
    core, z, x = info_ref[3], info_ref[4], info_ref[5]
    copies = []
    for second in range(1, RING):
        for step in range(STEPS):
            for first in range(RING):
                group = origin(core, z, x, first, 0)
                tile = needs_ref[info_ref[step], second * 16 + group]
                copies.append(pltpu.make_async_copy(
                    held[first].at[step, tile], sent[second - 1].at[step, first], sems.at[len(copies)]))
                copies[-1].start()
    for copy in copies:
        copy.wait()


def pick(needs, info, held):
    steps, _, rows, width = held[0].shape
    shape = jax.ShapeDtypeStruct((steps, RING, rows, width), held[0].dtype)
    return pl.pallas_call(
        pick_kernel,
        in_specs=[pl.BlockSpec(memory_space=pltpu.SMEM)] * 2 + [pl.BlockSpec(memory_space=pltpu.VMEM)] * RING,
        out_specs=[pl.BlockSpec(memory_space=pl.ANY)] * (RING - 1),
        out_shape=[shape] * (RING - 1),
        scratch_shapes=[pltpu.SemaphoreType.DMA((steps * (RING - 1) * RING,))],
        compiler_params=pltpu.CompilerParams(vmem_limit_bytes=8 << 20),
        cost_estimate=pl.CostEstimate(flops=27600000000, bytes_accessed=8 << 20, transcendentals=0),
        name="pick",
    )(needs, info, *held)


def ladder_kernel(needs_ref, info_ref, *refs):
    halves, refs = refs[:10], refs[10:]
    held, blocks, (out_ref, lefts, rights, total, left_sems, right_sems, out_sems) = (
        refs[:RING], refs[RING:2 * RING - 1], refs[2 * RING - 1:])
    chip, core, z, x = (info_ref[2] >> 1), info_ref[3], info_ref[4], info_ref[5]
    each = halves[0].shape[1]
    parts = total.shape[0]

    def left(source, step, group):
        start = pl.multiple_of(group * TW, TW)
        return pltpu.make_async_copy(source, lefts.at[step, :, pl.ds(start, TW)], left_sems.at[step, group])

    def slot_of(group):
        back_z, back_x = wrap(z - (group >> 2)), wrap(x - group)
        return jnp.where(core == 0, back_x * RING + back_z, back_z * RING + back_x)

    def right(source, step, second, first=0, count=RING):
        return pltpu.make_async_copy(
            source, rights.at[step, pl.ds((second * RING + first) * TW, count * TW)], right_sems.at[step, second])

    def block(step, second):
        return blocks[second - 1].at[step]

    for step in range(STEPS):
        for place, half in enumerate((core, 1 - core)):
            for shift in range(RING):
                for inner in range(each):
                    group = (wrap(chip - shift) * 2 + half) * each + inner
                    part = halves[place * 5 + (0, 1, 3 + step, 2)[shift]]
                    left(part.at[inner] if shift == 2 else part.at[step, inner], step, slot_of(group)).start()
        for first in range(RING):
            tile = needs_ref[info_ref[step], origin(core, z, x, first, 0)]
            right(held[first].at[step, tile], step, 0, first, 1).start()
        for second in range(1, RING):
            right(block(step, second), step, second).start()

    for step, start, stop in ((0, 0, RING), (1, 0, RING)):
        for second in range(start, stop):
            for first in range(RING):
                left(halves[0].at[step, 0], step, second * RING + first).wait()
            right(block(step, 1), step, second).wait()

        @pl.loop(0, parts)
        def _(part):
            span = pl.ds(pl.multiple_of(part * PART, PART), PART)
            depth = slice(start * RING * TW, stop * RING * TW)
            product = jnp.dot(lefts[step, :, depth], rights[step, depth, span], preferred_element_type=jnp.float32)
            total[part] = product if step == 0 and start == 0 else total[part] + product
            if step == STEPS - 1:
                pltpu.make_async_copy(total.at[part], out_ref.at[:, span], out_sems.at[part]).start()

    for part in range(parts):
        pltpu.make_async_copy(total.at[part], out_ref.at[:, pl.ds(part * PART, PART)], out_sems.at[part]).wait()


def multiply(needs, info, halves, held, blocks):
    steps, each, rows, _ = halves[0].shape
    groups = 2 * RING * each
    depth, width = groups * TW, held[0].shape[-1]
    kind = held[0].dtype
    return pl.pallas_call(
        ladder_kernel,
        in_specs=[pl.BlockSpec(memory_space=pltpu.SMEM)] * 2
        + [pl.BlockSpec(memory_space=pl.ANY)] * (len(halves) + len(held) + len(blocks)),
        out_specs=pl.BlockSpec(memory_space=pl.ANY),
        out_shape=jax.ShapeDtypeStruct((rows, width), jnp.float32),
        scratch_shapes=[pltpu.VMEM((steps, rows, depth), kind),
                        pltpu.VMEM((steps, depth, width), kind),
                        pltpu.VMEM((width // PART, rows, PART), jnp.float32),
                        pltpu.SemaphoreType.DMA((steps, groups)),
                        pltpu.SemaphoreType.DMA((steps, RING)),
                        pltpu.SemaphoreType.DMA((width // PART,))],
        compiler_params=pltpu.CompilerParams(vmem_limit_bytes=28 << 20),
        cost_estimate=pl.CostEstimate(flops=2 * rows * steps * depth * width, bytes_accessed=24 << 20, transcendentals=0),
        name="ladder",
    )(needs, info, *halves, *held, *[block.reshape(steps, RING * TW, width) for block in blocks])


def local(amplitudes, amp_mask, integrals, int_mask, steps):
    tiles, ab_width = integrals.shape[1] // TW, integrals.shape[2]
    row = lax.axis_index(ROW)
    core, z, x = (lax.axis_index(axis) for axis in GRID)
    info = jnp.stack([steps[0], steps[1], row, core, z, x]).astype(jnp.int32)

    own = jnp.max(amp_mask, axis=0).reshape(1, -1, 2)[:, :, 1]
    by_row = lax.all_to_all(jnp.broadcast_to(own, (ROWS, own.shape[1])), ROW, 0, 0, tiled=True)
    readers = [by_row] + [lax.ppermute(by_row, GRID, plane_perm(False, RING - ahead)) for ahead in (1, 2, 3)]
    needs = jnp.concatenate(readers, axis=1)

    gate = int_mask.astype(integrals.dtype)[:, :, None, :, None]
    block = integrals.reshape(STEPS, tiles, TW, ab_width // TW, TW) * gate
    block = block.reshape(STEPS, tiles, TW, ab_width)
    held = [block] + [lax.ppermute(block, GRID, plane_perm(True, shift)) for shift in (1, 2, 3)]

    sent = pick(needs, info, held)
    pieces = lax.all_to_all(compress(amplitudes, amp_mask), ROW, 0, 0, tiled=True)
    each = pieces.shape[0] // ROWS
    halves = [jnp.stack([lax.dynamic_slice_in_dim(pieces, steps[step] * each, each, 0) for step in range(STEPS)])]
    halves += [lax.ppermute(halves[0], "y", round_y(shift)) for shift in (1, 3)]
    halves += [lax.ppermute(halves[1][0], "y", round_y(1)), lax.ppermute(halves[2][1], "y", round_y(3))]
    halves += [lax.ppermute(half, "core", [(0, 1), (1, 0)]) for half in halves]

    blocks = [lax.ppermute(sent[shift - 1], GRID, plane_perm(False, shift)) for shift in (1, 2, 3)]
    return multiply(needs, info, halves, held, blocks)


def solution(mesh):
    grid = Mesh(mesh.devices.reshape(4, 2, 4, 4), ("y", "core", "z", "x"))
    return jax.shard_map(
        local,
        mesh=grid,
        in_specs=(P(COL, ROW), P(COL, ROW), P(None, COL, ROW), P(None, COL, ROW), P()),
        out_specs=P(COL, ROW),
        check_vma=False,
    )
```

```python
import functools

import jax
import jax.numpy as jnp
from jax import lax
from jax.experimental import pallas as pl
from jax.experimental.pallas import tpu as pltpu
from jax.sharding import Mesh
from jax.sharding import PartitionSpec as P

TW = 128
PART = 256
STEPS = 2
RING = 4
ROWS = 8
ROW = ("y", "core")
COL = ("z", "x")
GRID = ("core", "z", "x")


def plane_perm(first, shift):
    pairs = []
    for core in range(2):
        for z in range(RING):
            for x in range(RING):
                along_z = (core == 0) == first
                to_z, to_x = ((z + shift) % RING, x) if along_z else (z, (x + shift) % RING)
                pairs.append((core * 16 + z * RING + x, core * 16 + to_z * RING + to_x))
    return pairs


def round_y(shift):
    return [(chip, (chip + shift) % RING) for chip in range(RING)]


def wrap(value):
    return value & (RING - 1)


def origin(core, z, x, first_shift, second_shift):
    on_zero = wrap(z - first_shift) * RING + wrap(x - second_shift)
    on_one = wrap(z - second_shift) * RING + wrap(x - first_shift)
    return jnp.where(core == 0, on_zero, on_one)


def needed_tile(mask_ref, group):
    found = mask_ref[0, 2 * group + 1]
    for row in range(1, 8):
        found = found | mask_ref[row, 2 * group + 1]
    return jnp.where(found != 0, 1, 0)


def column_loads(mask_ref, amp_ref, held, sems, groups):
    loads, columns = [], []
    for place, group in enumerate(groups):
        column = 2 * group + needed_tile(mask_ref, group)
        columns.append(column)
        loads.append(pltpu.make_async_copy(
            amp_ref.at[:, pl.ds(pl.multiple_of(column * TW, TW), TW)], held.at[place], sems.at[place]))
        loads[place].start()
    return loads, columns


def apply_mask(mask_ref, held, place, column):
    for tile in range(held.shape[1] // TW):
        span = slice(tile * TW, (tile + 1) * TW)

        @pl.when(mask_ref[tile, column] == 0)
        def _():
            held[place, span, :] = jnp.zeros((TW, TW), held.dtype)


def compress_kernel(mask_ref, amp_ref, out_ref, held, in_sems, out_sems):
    groups = held.shape[0]
    loads, columns = column_loads(mask_ref, amp_ref, held, in_sems, range(groups))
    stores = []
    for group, load in enumerate(loads):
        load.wait()
        apply_mask(mask_ref, held, group, columns[group])
        stores.append(pltpu.make_async_copy(held.at[group], out_ref.at[group], out_sems.at[group]))
        stores[-1].start()
    for store in stores:
        store.wait()


def compress(amplitudes, amp_mask):
    rows, groups = amplitudes.shape[0], amp_mask.shape[1] // 2
    kind = amplitudes.dtype
    return pl.pallas_call(
        compress_kernel,
        in_specs=[pl.BlockSpec(memory_space=pltpu.SMEM), pl.BlockSpec(memory_space=pl.ANY)],
        out_specs=pl.BlockSpec(memory_space=pl.ANY),
        out_shape=jax.ShapeDtypeStruct((groups, rows, TW), kind),
        scratch_shapes=[pltpu.VMEM((groups, rows, TW), kind),
                        pltpu.SemaphoreType.DMA((groups,)), pltpu.SemaphoreType.DMA((groups,))],
        compiler_params=pltpu.CompilerParams(vmem_limit_bytes=54 << 20),
        name="compress",
    )(amp_mask, amplitudes)


def gate_kernel(mask_ref, gate_ref, int_ref, block_ref, own_ref, held, in_sems, out_sems):
    steps, tiles, rows, width = held.shape
    loads, stores = [], []
    for step in range(steps):
        for tile in range(tiles):
            loads.append(pltpu.make_async_copy(
                int_ref.at[step, tile], held.at[step, tile], in_sems.at[step, tile]))
            loads[-1].start()
    lane = lax.broadcasted_iota(jnp.int32, own_ref.shape, 1)
    own = jnp.zeros(own_ref.shape, jnp.int32)
    for group in range(own_ref.shape[1]):
        own = jnp.where(lane == group, needed_tile(mask_ref, group), own)
    own_ref[...] = own
    for step in range(steps):
        for tile in range(tiles):
            loads[step * tiles + tile].wait()
            for place in range(width // TW):
                @pl.when(gate_ref[step, tile, place] == 0)
                def _():
                    held[step, tile, :, place * TW:(place + 1) * TW] = jnp.zeros((rows, TW), held.dtype)
            stores.append(pltpu.make_async_copy(
                held.at[step, tile], block_ref.at[step, tile], out_sems.at[step, tile]))
            stores[-1].start()
    for store in stores:
        store.wait()


def gate(amp_mask, integrals, int_mask):
    groups = amp_mask.shape[1] // 2
    return pl.pallas_call(
        gate_kernel,
        in_specs=[pl.BlockSpec(memory_space=pltpu.SMEM)] * 2 + [pl.BlockSpec(memory_space=pl.ANY)],
        out_specs=[pl.BlockSpec(memory_space=pl.ANY), pl.BlockSpec(memory_space=pltpu.VMEM)],
        out_shape=[jax.ShapeDtypeStruct(integrals.shape, integrals.dtype),
                   jax.ShapeDtypeStruct((ROWS, groups), jnp.int32)],
        scratch_shapes=[pltpu.VMEM(integrals.shape, integrals.dtype),
                        pltpu.SemaphoreType.DMA(int_mask.shape[:2]), pltpu.SemaphoreType.DMA(int_mask.shape[:2])],
        compiler_params=pltpu.CompilerParams(vmem_limit_bytes=60 << 20),
        name="gate",
    )(amp_mask, int_mask, integrals)


def pick_kernel(needs_ref, info_ref, *refs):
    held, sent, sems = refs[:RING], refs[RING:2 * RING - 1], refs[2 * RING - 1]
    core, z, x = info_ref[3], info_ref[4], info_ref[5]
    copies = []
    for second in range(1, RING):
        for step in range(STEPS):
            for first in range(RING):
                group = origin(core, z, x, first, 0)
                tile = needs_ref[info_ref[step], second * 16 + group]
                copies.append(pltpu.make_async_copy(
                    held[first].at[step, tile], sent[second - 1].at[step, first], sems.at[len(copies)]))
                copies[-1].start()
    for copy in copies:
        copy.wait()


def pick(needs, info, held):
    steps, _, rows, width = held[0].shape
    shape = jax.ShapeDtypeStruct((steps, RING, rows, width), held[0].dtype)
    return pl.pallas_call(
        pick_kernel,
        in_specs=[pl.BlockSpec(memory_space=pltpu.SMEM)] * 2 + [pl.BlockSpec(memory_space=pltpu.VMEM)] * RING,
        out_specs=[pl.BlockSpec(memory_space=pl.ANY)] * (RING - 1),
        out_shape=[shape] * (RING - 1),
        scratch_shapes=[pltpu.SemaphoreType.DMA((steps * (RING - 1) * RING,))],
        compiler_params=pltpu.CompilerParams(vmem_limit_bytes=8 << 20),
        cost_estimate=pl.CostEstimate(flops=27600000000, bytes_accessed=8 << 20, transcendentals=0),
        name="pick",
    )(needs, info, *held)


def ladder_kernel(needs_ref, info_ref, *refs):
    halves, refs = refs[:10], refs[10:]
    held, blocks, (out_ref, lefts, rights, total, left_sems, right_sems, out_sems) = (
        refs[:RING], refs[RING:2 * RING - 1], refs[2 * RING - 1:])
    chip, core, z, x = (info_ref[2] >> 1), info_ref[3], info_ref[4], info_ref[5]
    each = halves[0].shape[1]
    parts = total.shape[0]

    def left(source, step, group):
        start = pl.multiple_of(group * TW, TW)
        return pltpu.make_async_copy(source, lefts.at[step, :, pl.ds(start, TW)], left_sems.at[step, group])

    def slot_of(group):
        back_z, back_x = wrap(z - (group >> 2)), wrap(x - group)
        return jnp.where(core == 0, back_x * RING + back_z, back_z * RING + back_x)

    def right(source, step, second, first=0, count=RING):
        return pltpu.make_async_copy(
            source, rights.at[step, pl.ds((second * RING + first) * TW, count * TW)], right_sems.at[step, second])

    def block(step, second):
        return blocks[second - 1].at[step]

    for step in range(STEPS):
        for place, half in enumerate((core, 1 - core)):
            for shift in range(RING):
                for inner in range(each):
                    group = (wrap(chip - shift) * 2 + half) * each + inner
                    part = halves[place * 5 + (0, 1, 3 + step, 2)[shift]]
                    left(part.at[inner] if shift == 2 else part.at[step, inner], step, slot_of(group)).start()
        for first in range(RING):
            tile = needs_ref[info_ref[step], origin(core, z, x, first, 0)]
            right(held[first].at[step, tile], step, 0, first, 1).start()
        for second in range(1, RING):
            right(block(step, second), step, second).start()

    for step, start, stop in ((0, 0, RING), (1, 0, RING)):
        for second in range(start, stop):
            for first in range(RING):
                left(halves[0].at[step, 0], step, second * RING + first).wait()
            right(block(step, 1), step, second).wait()

        @pl.loop(0, parts)
        def _(part):
            span = pl.ds(pl.multiple_of(part * PART, PART), PART)
            depth = slice(start * RING * TW, stop * RING * TW)
            product = jnp.dot(lefts[step, :, depth], rights[step, depth, span], preferred_element_type=jnp.float32)
            total[part] = product if step == 0 and start == 0 else total[part] + product
            if step == STEPS - 1:
                pltpu.make_async_copy(total.at[part], out_ref.at[:, span], out_sems.at[part]).start()

    for part in range(parts):
        pltpu.make_async_copy(total.at[part], out_ref.at[:, pl.ds(part * PART, PART)], out_sems.at[part]).wait()


def multiply(needs, info, halves, held, blocks):
    steps, each, rows, _ = halves[0].shape
    groups = 2 * RING * each
    depth, width = groups * TW, held[0].shape[-1]
    kind = held[0].dtype
    return pl.pallas_call(
        ladder_kernel,
        in_specs=[pl.BlockSpec(memory_space=pltpu.SMEM)] * 2
        + [pl.BlockSpec(memory_space=pl.ANY)] * (len(halves) + len(held) + len(blocks)),
        out_specs=pl.BlockSpec(memory_space=pl.ANY),
        out_shape=jax.ShapeDtypeStruct((rows, width), jnp.float32),
        scratch_shapes=[pltpu.VMEM((steps, rows, depth), kind),
                        pltpu.VMEM((steps, depth, width), kind),
                        pltpu.VMEM((width // PART, rows, PART), jnp.float32),
                        pltpu.SemaphoreType.DMA((steps, groups)),
                        pltpu.SemaphoreType.DMA((steps, RING)),
                        pltpu.SemaphoreType.DMA((width // PART,))],
        compiler_params=pltpu.CompilerParams(vmem_limit_bytes=28 << 20),
        cost_estimate=pl.CostEstimate(flops=2 * rows * steps * depth * width, bytes_accessed=24 << 20, transcendentals=0),
        name="ladder",
    )(needs, info, *halves, *held, *[block.reshape(steps, RING * TW, width) for block in blocks])


def local(amplitudes, amp_mask, integrals, int_mask, steps):
    tiles, ab_width = integrals.shape[1] // TW, integrals.shape[2]
    row = lax.axis_index(ROW)
    core, z, x = (lax.axis_index(axis) for axis in GRID)
    info = jnp.stack([steps[0], steps[1], row, core, z, x]).astype(jnp.int32)

    block, own = gate(amp_mask, integrals.reshape(STEPS, tiles, TW, ab_width), int_mask)

    by_row = lax.all_to_all(own, ROW, 0, 0, tiled=True)
    readers = [by_row] + [lax.ppermute(by_row, GRID, plane_perm(False, RING - ahead)) for ahead in (1, 2, 3)]
    needs = jnp.concatenate(readers, axis=1)

    held = [block] + [lax.ppermute(block, GRID, plane_perm(True, shift)) for shift in (1, 2, 3)]

    sent = pick(needs, info, held)
    pieces = lax.all_to_all(compress(amplitudes, amp_mask), ROW, 0, 0, tiled=True)
    each = pieces.shape[0] // ROWS
    halves = [jnp.stack([lax.dynamic_slice_in_dim(pieces, steps[step] * each, each, 0) for step in range(STEPS)])]
    halves += [lax.ppermute(halves[0], "y", round_y(shift)) for shift in (1, 3)]
    halves += [lax.ppermute(halves[1][0], "y", round_y(1)), lax.ppermute(halves[2][1], "y", round_y(3))]
    halves += [lax.ppermute(half, "core", [(0, 1), (1, 0)]) for half in halves]

    blocks = [lax.ppermute(sent[shift - 1], GRID, plane_perm(False, shift)) for shift in (1, 2, 3)]
    return multiply(needs, info, halves, held, blocks)


def solution(mesh):
    grid = Mesh(mesh.devices.reshape(4, 2, 4, 4), ("y", "core", "z", "x"))
    return jax.shard_map(
        local,
        mesh=grid,
        in_specs=(P(COL, ROW), P(COL, ROW), P(None, COL, ROW), P(None, COL, ROW), P()),
        out_specs=P(COL, ROW),
        check_vma=False,
    )
```

```python
import functools

import jax
import jax.numpy as jnp
from jax import lax
from jax.experimental import pallas as pl
from jax.experimental.pallas import tpu as pltpu
from jax.sharding import Mesh
from jax.sharding import PartitionSpec as P

TW = 128
PART = 256
STEPS = 2
RING = 4
ROWS = 8
ROW = ("y", "core")
COL = ("z", "x")
GRID = ("core", "z", "x")


def plane_perm(first, shift):
    pairs = []
    for core in range(2):
        for z in range(RING):
            for x in range(RING):
                along_z = (core == 0) == first
                to_z, to_x = ((z + shift) % RING, x) if along_z else (z, (x + shift) % RING)
                pairs.append((core * 16 + z * RING + x, core * 16 + to_z * RING + to_x))
    return pairs


def round_y(shift):
    return [(chip, (chip + shift) % RING) for chip in range(RING)]


def wrap(value):
    return value & (RING - 1)


def origin(core, z, x, first_shift, second_shift):
    on_zero = wrap(z - first_shift) * RING + wrap(x - second_shift)
    on_one = wrap(z - second_shift) * RING + wrap(x - first_shift)
    return jnp.where(core == 0, on_zero, on_one)


def needed_tile(mask_ref, group):
    found = mask_ref[0, 2 * group + 1]
    for row in range(1, 8):
        found = found | mask_ref[row, 2 * group + 1]
    return jnp.where(found != 0, 1, 0)


def column_loads(mask_ref, amp_ref, held, sems, groups):
    loads, columns = [], []
    for place, group in enumerate(groups):
        column = 2 * group + needed_tile(mask_ref, group)
        columns.append(column)
        loads.append(pltpu.make_async_copy(
            amp_ref.at[:, pl.ds(pl.multiple_of(column * TW, TW), TW)], held.at[place], sems.at[place]))
        loads[place].start()
    return loads, columns


def apply_mask(mask_ref, held, place, column):
    for tile in range(held.shape[1] // TW):
        span = slice(tile * TW, (tile + 1) * TW)

        @pl.when(mask_ref[tile, column] == 0)
        def _():
            held[place, span, :] = jnp.zeros((TW, TW), held.dtype)


def compress_kernel(mask_ref, amp_ref, out_ref, held, in_sems, out_sems):
    groups = held.shape[0]
    loads, columns = column_loads(mask_ref, amp_ref, held, in_sems, range(groups))
    stores = []
    for group, load in enumerate(loads):
        load.wait()
        apply_mask(mask_ref, held, group, columns[group])
        stores.append(pltpu.make_async_copy(held.at[group], out_ref.at[group], out_sems.at[group]))
        stores[-1].start()
    for store in stores:
        store.wait()


def compress(amplitudes, amp_mask):
    rows, groups = amplitudes.shape[0], amp_mask.shape[1] // 2
    kind = amplitudes.dtype
    return pl.pallas_call(
        compress_kernel,
        in_specs=[pl.BlockSpec(memory_space=pltpu.SMEM), pl.BlockSpec(memory_space=pl.ANY)],
        out_specs=pl.BlockSpec(memory_space=pl.ANY),
        out_shape=jax.ShapeDtypeStruct((groups, rows, TW), kind),
        scratch_shapes=[pltpu.VMEM((groups, rows, TW), kind),
                        pltpu.SemaphoreType.DMA((groups,)), pltpu.SemaphoreType.DMA((groups,))],
        compiler_params=pltpu.CompilerParams(vmem_limit_bytes=54 << 20),
        name="compress",
    )(amp_mask, amplitudes)


def gate_kernel(mask_ref, gate_ref, int_ref, block_ref, own_ref, in_sems):
    steps, tiles, rows, width = block_ref.shape
    loads = []
    for step in range(steps):
        for tile in range(tiles):
            loads.append(pltpu.make_async_copy(
                int_ref.at[step, tile], block_ref.at[step, tile], in_sems.at[step, tile]))
            loads[-1].start()
    lane = lax.broadcasted_iota(jnp.int32, own_ref.shape, 1)
    own = jnp.zeros(own_ref.shape, jnp.int32)
    for group in range(own_ref.shape[1]):
        own = jnp.where(lane == group, needed_tile(mask_ref, group), own)
    own_ref[...] = own
    for step in range(steps):
        for tile in range(tiles):
            loads[step * tiles + tile].wait()
            for place in range(width // TW):
                @pl.when(gate_ref[step, tile, place] == 0)
                def _():
                    block_ref[step, tile, :, place * TW:(place + 1) * TW] = jnp.zeros((rows, TW), block_ref.dtype)


def gate(amp_mask, integrals, int_mask):
    groups = amp_mask.shape[1] // 2
    return pl.pallas_call(
        gate_kernel,
        in_specs=[pl.BlockSpec(memory_space=pltpu.SMEM)] * 2 + [pl.BlockSpec(memory_space=pl.ANY)],
        out_specs=[pl.BlockSpec(memory_space=pltpu.VMEM)] * 2,
        out_shape=[jax.ShapeDtypeStruct(integrals.shape, integrals.dtype),
                   jax.ShapeDtypeStruct((ROWS, groups), jnp.int32)],
        scratch_shapes=[pltpu.SemaphoreType.DMA(int_mask.shape[:2])],
        compiler_params=pltpu.CompilerParams(vmem_limit_bytes=60 << 20),
        name="gate",
    )(amp_mask, int_mask, integrals)


def pick_kernel(needs_ref, info_ref, *refs):
    held, sent, sems = refs[:RING], refs[RING:2 * RING - 1], refs[2 * RING - 1]
    core, z, x = info_ref[3], info_ref[4], info_ref[5]
    copies = []
    for second in range(1, RING):
        for step in range(STEPS):
            for first in range(RING):
                group = origin(core, z, x, first, 0)
                tile = needs_ref[info_ref[step], second * 16 + group]
                copies.append(pltpu.make_async_copy(
                    held[first].at[step, tile], sent[second - 1].at[step, first], sems.at[len(copies)]))
                copies[-1].start()
    for copy in copies:
        copy.wait()


def pick(needs, info, held):
    steps, _, rows, width = held[0].shape
    shape = jax.ShapeDtypeStruct((steps, RING, rows, width), held[0].dtype)
    return pl.pallas_call(
        pick_kernel,
        in_specs=[pl.BlockSpec(memory_space=pltpu.SMEM)] * 2 + [pl.BlockSpec(memory_space=pltpu.VMEM)] * RING,
        out_specs=[pl.BlockSpec(memory_space=pl.ANY)] * (RING - 1),
        out_shape=[shape] * (RING - 1),
        scratch_shapes=[pltpu.SemaphoreType.DMA((steps * (RING - 1) * RING,))],
        compiler_params=pltpu.CompilerParams(vmem_limit_bytes=8 << 20),
        cost_estimate=pl.CostEstimate(flops=27600000000, bytes_accessed=8 << 20, transcendentals=0),
        name="pick",
    )(needs, info, *held)


def ladder_kernel(needs_ref, info_ref, *refs):
    halves, refs = refs[:10], refs[10:]
    held, blocks, (out_ref, lefts, rights, total, left_sems, right_sems, out_sems) = (
        refs[:RING], refs[RING:2 * RING - 1], refs[2 * RING - 1:])
    chip, core, z, x = (info_ref[2] >> 1), info_ref[3], info_ref[4], info_ref[5]
    each = halves[0].shape[1]
    parts = total.shape[0]

    def left(source, step, group):
        start = pl.multiple_of(group * TW, TW)
        return pltpu.make_async_copy(source, lefts.at[step, :, pl.ds(start, TW)], left_sems.at[step, group])

    def slot_of(group):
        back_z, back_x = wrap(z - (group >> 2)), wrap(x - group)
        return jnp.where(core == 0, back_x * RING + back_z, back_z * RING + back_x)

    def right(source, step, second, first=0, count=RING):
        return pltpu.make_async_copy(
            source, rights.at[step, pl.ds((second * RING + first) * TW, count * TW)], right_sems.at[step, second])

    def block(step, second):
        return blocks[second - 1].at[step]

    for step in range(STEPS):
        for place, half in enumerate((core, 1 - core)):
            for shift in range(RING):
                for inner in range(each):
                    group = (wrap(chip - shift) * 2 + half) * each + inner
                    part = halves[place * 5 + (0, 1, 3 + step, 2)[shift]]
                    left(part.at[inner] if shift == 2 else part.at[step, inner], step, slot_of(group)).start()
        for first in range(RING):
            tile = needs_ref[info_ref[step], origin(core, z, x, first, 0)]
            right(held[first].at[step, tile], step, 0, first, 1).start()
        for second in range(1, RING):
            right(block(step, second), step, second).start()

    for step, start, stop in ((0, 0, RING), (1, 0, RING)):
        for second in range(start, stop):
            for first in range(RING):
                left(halves[0].at[step, 0], step, second * RING + first).wait()
            right(block(step, 1), step, second).wait()

        @pl.loop(0, parts)
        def _(part):
            span = pl.ds(pl.multiple_of(part * PART, PART), PART)
            depth = slice(start * RING * TW, stop * RING * TW)
            product = jnp.dot(lefts[step, :, depth], rights[step, depth, span], preferred_element_type=jnp.float32)
            total[part] = product if step == 0 and start == 0 else total[part] + product
            if step == STEPS - 1:
                pltpu.make_async_copy(total.at[part], out_ref.at[:, span], out_sems.at[part]).start()

    for part in range(parts):
        pltpu.make_async_copy(total.at[part], out_ref.at[:, pl.ds(part * PART, PART)], out_sems.at[part]).wait()


def multiply(needs, info, halves, held, blocks):
    steps, each, rows, _ = halves[0].shape
    groups = 2 * RING * each
    depth, width = groups * TW, held[0].shape[-1]
    kind = held[0].dtype
    return pl.pallas_call(
        ladder_kernel,
        in_specs=[pl.BlockSpec(memory_space=pltpu.SMEM)] * 2
        + [pl.BlockSpec(memory_space=pl.ANY)] * (len(halves) + len(held) + len(blocks)),
        out_specs=pl.BlockSpec(memory_space=pl.ANY),
        out_shape=jax.ShapeDtypeStruct((rows, width), jnp.float32),
        scratch_shapes=[pltpu.VMEM((steps, rows, depth), kind),
                        pltpu.VMEM((steps, depth, width), kind),
                        pltpu.VMEM((width // PART, rows, PART), jnp.float32),
                        pltpu.SemaphoreType.DMA((steps, groups)),
                        pltpu.SemaphoreType.DMA((steps, RING)),
                        pltpu.SemaphoreType.DMA((width // PART,))],
        compiler_params=pltpu.CompilerParams(vmem_limit_bytes=28 << 20),
        cost_estimate=pl.CostEstimate(flops=2 * rows * steps * depth * width, bytes_accessed=24 << 20, transcendentals=0),
        name="ladder",
    )(needs, info, *halves, *held, *[block.reshape(steps, RING * TW, width) for block in blocks])


def local(amplitudes, amp_mask, integrals, int_mask, steps):
    tiles, ab_width = integrals.shape[1] // TW, integrals.shape[2]
    row = lax.axis_index(ROW)
    core, z, x = (lax.axis_index(axis) for axis in GRID)
    info = jnp.stack([steps[0], steps[1], row, core, z, x]).astype(jnp.int32)

    block, own = gate(amp_mask, integrals.reshape(STEPS, tiles, TW, ab_width), int_mask)

    by_row = lax.all_to_all(own, ROW, 0, 0, tiled=True)
    readers = [by_row] + [lax.ppermute(by_row, GRID, plane_perm(False, RING - ahead)) for ahead in (1, 2, 3)]
    needs = jnp.concatenate(readers, axis=1)

    held = [block] + [lax.ppermute(block, GRID, plane_perm(True, shift)) for shift in (1, 2, 3)]

    sent = pick(needs, info, held)
    pieces = lax.all_to_all(compress(amplitudes, amp_mask), ROW, 0, 0, tiled=True)
    each = pieces.shape[0] // ROWS
    halves = [jnp.stack([lax.dynamic_slice_in_dim(pieces, steps[step] * each, each, 0) for step in range(STEPS)])]
    halves += [lax.ppermute(halves[0], "y", round_y(shift)) for shift in (1, 3)]
    halves += [lax.ppermute(halves[1][0], "y", round_y(1)), lax.ppermute(halves[2][1], "y", round_y(3))]
    halves += [lax.ppermute(half, "core", [(0, 1), (1, 0)]) for half in halves]

    blocks = [lax.ppermute(sent[shift - 1], GRID, plane_perm(False, shift)) for shift in (1, 2, 3)]
    return multiply(needs, info, halves, held, blocks)


def solution(mesh):
    grid = Mesh(mesh.devices.reshape(4, 2, 4, 4), ("y", "core", "z", "x"))
    return jax.shard_map(
        local,
        mesh=grid,
        in_specs=(P(COL, ROW), P(COL, ROW), P(None, COL, ROW), P(None, COL, ROW), P()),
        out_specs=P(COL, ROW),
        check_vma=False,
    )
```
